512 devices in a mesh: al: 32 (over y, x), ka: 16 (over z, core).
Axes of the slice: x: 4, y: 8, z: 8, core: 2. Of those that a mesh axis runs over, the one named last changes fastest.
Arguments:
- amplitudes: float32 [128, 2048, 128], P('al', 'ka'), may hold values from -6 to 6
- kernel: bfloat16 [128, 2048, 2048], P('al', 'ka'), as said below
- block_lengths: int32 [32], P('al'), may hold values from 1 to 4, 64 in all
- m_counts: int32 [64], replicated, may hold values from 1 to 64, as said below
- vector_potential: float32 [2, 2], replicated, may hold values from -2 to 2
Outputs:
- advanced: float32 [128, 2048, 128], P('al', 'ka')
The draws below stay inside these ranges and needn't reach their ends.
Inputs may be any that keep to these rules, and one draw needn't show every extreme that they name: `block_lengths`: the lengths sum to 64; one of them equals 4. `m_counts`: the count of partial wave l is at most 2 l + 1; the last partial wave has the largest count. Each slot's kernel is exactly symmetric in its two momenta.
All inputs are finite; a program needn't handle non-finite values. No bound on the sum of `block_lengths` on one device may be relied on, other than what follows from the above.
Results may differ from the reference program's by a relative error of at most 0.007.
Values may be sent and summed in bfloat16 or wider, within the bound.
No kernel may reach another device: no remote copies, remote signals or barrier semaphores. Data moves between devices by JAX's collectives and lax.ppermute only.
A program may use at most 64 MiB of HBM per device.

```python
import math
import jax
import jax.numpy as jnp
import numpy as np
from jax import lax

MOMENTUM_POINTS = 2048
CHANNEL_CAPACITY = 64
LSLOT = 4
LMAX = 64
WAVE_SLOT_TOTAL = 128
N_AL = 32
N_KA = 16


def draw_kernel(key, part):
    key = jax.random.fold_in(key, 11)
    unsorted_sample = jax.random.normal(key, (WAVE_SLOT_TOTAL, MOMENTUM_POINTS, MOMENTUM_POINTS), jnp.float32)
    scaled = unsorted_sample * (2.0 / MOMENTUM_POINTS ** 0.5)
    symmetric = (scaled + jnp.swapaxes(scaled, 1, 2)) * 0.70710678
    return symmetric.astype(jnp.bfloat16)


def draw_m_counts(key, part):
    key = jax.random.fold_in(key, 23)
    waves_all = jnp.arange(LMAX, dtype=jnp.int32)
    ceiling = jnp.minimum(2 * waves_all + 1, CHANNEL_CAPACITY).astype(jnp.int32)
    drawn = jax.random.randint(key, (LMAX,), 1, ceiling + 1).astype(jnp.int32)
    return jnp.where(waves_all == LMAX - 1, ceiling, drawn).astype(jnp.int32)


def steps_of(rng, extent, pieces, smallest, high):
    factor_of = 1.0
    for dim, blocks in pieces:
        steps = jax.random.uniform(jax.random.fold_in(jax.random.fold_in(rng, 6), dim), (blocks,), jnp.float32, smallest / len(pieces), high / len(pieces))
        factor_of = factor_of * jnp.repeat(jnp.exp(steps), extent[dim] // blocks).reshape((-1,) + (1,) * (len(extent) - 1 - dim))
    return factor_of


def profile(number_of, total, limit, slope):
    weights = [(1 << 20) // math.isqrt(standing ** slope) + 1 for standing in range(2, number_of + 1)]
    surplus, holding = total - limit - (number_of - 1), [1] * (number_of - 1)
    while surplus > 0:
        movable = [i for i in range(number_of - 1) if holding[i] < limit]
        whole, left = sum([weights[i] for i in movable]), surplus
        for i in movable:
            addition = min(limit - holding[i], max(1, left * weights[i] // whole), surplus)
            holding[i] = holding[i] + addition
            surplus = surplus - addition
    return np.array([limit] + holding)


def uneven(stream_key, count, total, reach, slope):
    if count == 2:
        one = jax.random.randint(stream_key, (), max(1, total - reach), min(reach, total - 1) + 1)
        return jnp.stack([one, total - one])
    sizes = jnp.asarray(profile(count, total, reach, slope), jnp.int32)
    couples = (count - 1) // 2
    donor, taker = sizes[1:1 + 2 * couples:2], sizes[2:2 + 2 * couples:2]
    room = jnp.minimum(donor - 1, reach - taker)
    moved = jax.random.randint(jax.random.fold_in(stream_key, 1), (couples,), 0, 1 << 20) % (room + 1)
    sizes = sizes.at[1:1 + 2 * couples:2].set(donor - moved).at[2:2 + 2 * couples:2].set(taker + moved)
    return sizes[jax.random.permutation(jax.random.fold_in(stream_key, 2), count)]


def noise(stream_key, shape, spread, most, split=(), held_as=jnp.bfloat16):
    values = spread * jax.random.normal(stream_key, shape, jnp.float32)
    if split:
        values = values * steps_of(stream_key, shape, split, -0.22, 0.18)
    return jnp.clip(values, -most, most).astype(held_as)


def setup_inputs(seed: int = 0) -> dict:
    key_list = jax.random.split(jax.random.key(seed), 6)
    amplitudes = noise(key_list[0], (WAVE_SLOT_TOTAL, MOMENTUM_POINTS, 2 * CHANNEL_CAPACITY), 1.0, 6.0, ((0, 32), (1, 16)), jnp.float32)
    kernel = draw_kernel(jax.random.fold_in(key_list[5], 71), 0)
    block_lengths = uneven(key_list[2], N_AL, LMAX, LSLOT, 2).astype(jnp.int32)
    m_counts = draw_m_counts(jax.random.fold_in(key_list[5], 71), 0)
    vector_potential = jnp.clip(jax.random.uniform(key_list[4], (2, 2), jnp.float32, -2.0, 2.0), -2.0, 2.0)
    return dict(amplitudes=amplitudes, kernel=kernel, block_lengths=block_lengths, m_counts=m_counts, vector_potential=vector_potential)


step_length = 0.2
momentum_top = 3.0

def raising(upper_wave, lower_wave, m_low):
    lower_float = lower_wave.astype(jnp.float32)
    m_float = m_low.astype(jnp.float32)
    plus_term = (lower_float + m_float + 1.0) * (lower_float + m_float + 2.0) / jnp.maximum((2.0 * lower_float + 1.0) * (2.0 * lower_float + 3.0), 1.0)
    minus_term = jnp.maximum((lower_float - m_float) * (lower_float - m_float - 1.0), 0.0) / jnp.maximum((2.0 * lower_float - 1.0) * (2.0 * lower_float + 1.0), 1.0)
    return jnp.where(upper_wave == lower_wave + 1, jnp.sqrt(jnp.maximum(plus_term, 0.0)), jnp.where(upper_wave == lower_wave - 1, -jnp.sqrt(minus_term), 0.0))

def mix_block(wave_target, wave_source, count_target, count_source, field_x, field_y, mslots, lcount):
    target = jnp.arange(mslots, dtype=jnp.int32)[:, None]
    source = jnp.arange(mslots, dtype=jnp.int32)[None, :]
    m_target = target - (count_target - 1) // 2
    m_source = source - (count_source - 1) // 2
    allowed = (target < count_target) & (source < count_source) & (wave_source >= 0) & (wave_source < lcount)
    raise_part = jnp.where(allowed & (m_target == m_source + 1), raising(wave_target, wave_source, m_source), 0.0)
    lower_part = jnp.where(allowed & (m_target == m_source - 1), raising(wave_source, wave_target, m_target), 0.0)
    real_part = 0.5 * field_x * (raise_part + lower_part)
    imag_part = 0.5 * field_y * (lower_part - raise_part)
    top_half = jnp.concatenate([real_part.T, imag_part.T], axis=1)
    bottom_half = jnp.concatenate([-imag_part.T, real_part.T], axis=1)
    return jnp.concatenate([top_half, bottom_half], axis=0)

def reference(amplitudes, kernel, block_lengths, m_counts, vector_potential):
    waves_all = jnp.arange(LMAX, dtype=jnp.int32)
    block_ends = jnp.cumsum(block_lengths).astype(jnp.int32)
    block_starts = (block_ends - block_lengths).astype(jnp.int32)
    owner_device = lax.optimization_barrier(jnp.sum((waves_all[:, None] >= block_ends[None, :]).astype(jnp.int32), axis=1)).astype(jnp.int32)
    slot_lookup_for = (owner_device * LSLOT + waves_all - block_starts[owner_device]).astype(jnp.int32)
    lane_number = 2 * CHANNEL_CAPACITY
    block_size = MOMENTUM_POINTS // N_KA
    lane_keep = ((jnp.arange(lane_number, dtype=jnp.int32) % CHANNEL_CAPACITY)[None, :] < m_counts[:, None]).astype(jnp.float32)[:, None, :]
    start_state = amplitudes[slot_lookup_for] * lane_keep
    momenta = (jnp.arange(MOMENTUM_POINTS, dtype=jnp.float32) + 0.5) * (momentum_top / MOMENTUM_POINTS)
    below_index = jnp.clip(waves_all - 1, 0, LMAX - 1).astype(jnp.int32)
    above_index = jnp.clip(waves_all + 1, 0, LMAX - 1).astype(jnp.int32)
    build = jax.vmap(mix_block, in_axes=(0, 0, 0, 0, None, None, None, None))

    def time_derivative(current, field_x, field_y):
        rounded = current.astype(jnp.bfloat16)

        def one_wave(wave_index):
            kernel_blocks = kernel[slot_lookup_for[wave_index]].astype(jnp.float32).reshape(MOMENTUM_POINTS, N_KA, block_size)
            state_blocks = rounded[wave_index].astype(jnp.float32).reshape(N_KA, block_size, lane_number)
            parts = jnp.einsum('rbk,bkn->brn', kernel_blocks, state_blocks, precision=lax.Precision.HIGHEST)
            parts = lax.optimization_barrier(parts.astype(jnp.bfloat16)).astype(jnp.float32)
            return lax.optimization_barrier(jnp.sum(parts, axis=0))
        kernel_term = lax.map(one_wave, waves_all)
        lower_mix = build(waves_all, waves_all - 1, m_counts, m_counts[below_index], field_x, field_y, CHANNEL_CAPACITY, LMAX)
        upper_mix = build(waves_all, waves_all + 1, m_counts, m_counts[above_index], field_x, field_y, CHANNEL_CAPACITY, LMAX)
        coupled = jnp.einsum('lkn,lnp->lkp', current[below_index], lower_mix, precision=lax.Precision.HIGHEST)
        coupled = coupled + jnp.einsum('lkn,lnp->lkp', current[above_index], upper_mix, precision=lax.Precision.HIGHEST)
        hamiltonian = 0.5 * (momenta * momenta)[None, :, None] * current + kernel_term + momenta[None, :, None] * coupled
        return jnp.concatenate([hamiltonian[..., CHANNEL_CAPACITY:], -hamiltonian[..., :CHANNEL_CAPACITY]], axis=-1)
    half_state = start_state + 0.5 * step_length * time_derivative(start_state, vector_potential[0, 0], vector_potential[0, 1])
    ending_state = start_state + step_length * time_derivative(half_state, vector_potential[1, 0], vector_potential[1, 1])
    ending_state = ending_state * lane_keep
    return jnp.zeros((WAVE_SLOT_TOTAL, MOMENTUM_POINTS, lane_number), jnp.float32).at[slot_lookup_for].set(ending_state)
```

```python
import functools

import jax
import jax.numpy as jnp
from jax import lax
from jax.experimental import pallas as pl
from jax.experimental.pallas import tpu as pltpu
from jax.sharding import PartitionSpec as P

step_length = 0.2
momentum_top = 3.0
TOP = 13
VMEM_LIMIT = 32 * 1024 * 1024


def encode(rounded, out_ref, slot):
    rows, lanes = rounded.shape
    values = rounded.astype(jnp.float32)
    largest = jnp.max(jnp.abs(values), axis=0, keepdims=True)
    exponent = jnp.clip(jnp.floor(jnp.log2(jnp.maximum(largest, 1e-36))), -110.0, 127.0)
    scaled = values * jnp.exp2(TOP - exponent)
    out_ref[slot * rows : (slot + 1) * rows, :] = scaled.astype(out_ref.dtype)
    return exponent


def store_exponents(exponents, out_ref, start):
    lanes = exponents[0].shape[1]
    pad = out_ref.shape[0] - start - len(exponents)
    rows = jnp.concatenate(exponents + [jnp.zeros((pad, lanes), jnp.float32)], axis=0)
    out_ref[start:, :] = rows.astype(out_ref.dtype)


def encode_kernel(slots, held_ref, psi_ref, out_ref, low_ref, high_ref):
    rows = psi_ref.shape[1]
    exponents = []
    for slot in range(slots):
        rounded = psi_ref[slot].astype(jnp.bfloat16)
        exponents.append(encode(rounded, out_ref, slot))
    store_exponents(exponents, out_ref, slots * rows)
    low_ref[...] = psi_ref[0].astype(jnp.bfloat16)
    high_ref[...] = psi_ref[held_ref[0] - 1].astype(jnp.bfloat16)


def kernel_product(slot, slots, rows, blocks, gathered_ref, kernel_ref, scales):
    total = None
    for pair in range(0, blocks, 2):
        pieces = []
        for block in (pair, pair + 1):
            piece = gathered_ref[block, slot * rows : (slot + 1) * rows, :]
            scale = scales[block][slot : slot + 1]
            pieces.append((piece.astype(jnp.float32) * scale).astype(jnp.bfloat16))
        part = jnp.dot(
            kernel_ref[slot, :, pair * rows : (pair + 2) * rows],
            jnp.concatenate(pieces, axis=0),
            preferred_element_type=jnp.float32,
        )
        total = part if total is None else total + part
    return total


def read_scales(slots, rows, blocks, gathered_ref):
    start = slots * rows
    return [
        jnp.exp2(gathered_ref[b, start : start + 16, :].astype(jnp.float32) - TOP)
        for b in range(blocks)
    ]


def raise_to(v, n):
    return jnp.sqrt(
        jnp.maximum((v + n + 1.0) * (v + n + 2.0) / jnp.maximum((2.0 * v + 1.0) * (2.0 * v + 3.0), 1.0), 0.0)
    )


def drop_to(v, n):
    return -jnp.sqrt(
        jnp.maximum((v - n) * (v - n - 1.0), 0.0) / jnp.maximum((2.0 * v - 1.0) * (2.0 * v + 1.0), 1.0)
    )


def derivative(
    slot, first, held, waves, counts_ref, field_x, field_y, momenta, current, kernel_term, below, above
):
    rows, lanes = current.shape
    mslots = lanes // 2
    wave = first + slot
    low, high = wave - 1, wave + 1

    def count_of(index):
        return counts_ref[jnp.clip(index, 0, waves - 1)]

    count, count_low, count_high = count_of(wave), count_of(low), count_of(high)
    lane = lax.broadcasted_iota(jnp.int32, (1, lanes), 1)
    q = jnp.where(lane < mslots, lane, lane - mslots)
    m = (q - (count - 1) // 2).astype(jnp.float32)
    wave_f = wave.astype(jnp.float32)
    inside = q < count

    def moved(source, count_source, present, change, factor):
        shift = (count_source - 1) // 2 - (count - 1) // 2 - change
        p = q + shift
        allowed = inside & (p >= 0) & (p < count_source) & present
        turned = pltpu.roll(source, lax.rem(2 * lanes - shift, lanes), 1)
        return jnp.where(allowed, factor, 0.0) * turned

    has_low, has_high = low >= 0, high < waves
    up = moved(below, count_low, has_low, 1, raise_to(wave_f - 1.0, m - 1.0))
    up = up + moved(above, count_high, has_high, 1, drop_to(wave_f + 1.0, m - 1.0))
    down = moved(below, count_low, has_low, -1, drop_to(wave_f, m))
    down = down + moved(above, count_high, has_high, -1, raise_to(wave_f, m))
    turn = 0.5 * (momenta * momenta) * current + kernel_term + momenta * ((0.5 * field_x) * (up + down))
    swapped = pltpu.roll(turn, mslots, 1)
    swapped = jnp.where(lane < mslots, swapped, -swapped)
    flow = swapped + momenta * ((0.5 * field_y) * (down - up))
    return flow, inside & (slot < held)


def keep_of(slot, first, held, waves, counts_ref, lanes):
    count = counts_ref[jnp.clip(first + slot, 0, waves - 1)]
    lane = lax.broadcasted_iota(jnp.int32, (1, lanes), 1)
    q = jnp.where(lane < lanes // 2, lane, lane - lanes // 2)
    return (q < count) & (slot < held)


def momenta_of(place, rows, radial_count):
    row = lax.broadcasted_iota(jnp.int32, (rows, 1), 0) + place * rows
    return (row.astype(jnp.float32) + 0.5) * (momentum_top / radial_count)


def half_kernel(
    slots, waves, blocks, al_count,
    place_ref, held_ref, counts_ref, field_ref, psi_ref, gathered_ref, kernel_ref, below_ref, above_ref,
    half_ref, out_ref, low_ref, high_ref, first_ref,
):
    rows, lanes = psi_ref.shape[1:]
    al, ka = place_ref[0], place_ref[1]
    held = held_ref[0]
    start = slots * rows
    seen = None
    for block in range(blocks):
        row = gathered_ref[block, start : start + 16, :].astype(jnp.float32)[8:9]
        seen = row if seen is None else seen + row
    seen = jnp.max(seen).astype(jnp.int32)
    first = jnp.where(2 * al < al_count, seen, waves - held - seen)
    first_ref[0] = first
    momenta = momenta_of(ka, rows, kernel_ref.shape[2])
    scales = read_scales(slots, rows, blocks, gathered_ref)
    psi = [
        jnp.where(keep_of(s, first, held, waves, counts_ref, lanes), psi_ref[s], 0.0) for s in range(slots)
    ]
    lowest, highest = below_ref[...].astype(jnp.float32), above_ref[...].astype(jnp.float32)
    exponents = []
    for slot in range(slots):
        term = kernel_product(slot, slots, rows, blocks, gathered_ref, kernel_ref, scales)
        below = lowest if slot == 0 else psi[slot - 1]
        above = highest if slot == slots - 1 else jnp.where(slot + 1 < held, psi[slot + 1], highest)
        flow, keep = derivative(
            slot, first, held, waves, counts_ref, field_ref[0, 0], field_ref[0, 1], momenta,
            psi[slot], term, below, above,
        )
        half = jnp.where(keep, psi[slot] + (0.5 * step_length) * flow, 0.0)
        half_ref[slot] = half
        rounded = half.astype(jnp.bfloat16)
        exponents.append(encode(rounded, out_ref, slot))
        if slot == 0:
            low_ref[...] = rounded

        @pl.when(slot == held - 1)
        def _():
            high_ref[...] = rounded

    store_exponents(exponents, out_ref, start)


def product_kernel(slots, blocks, gathered_ref, kernel_ref, out_ref):
    rows = out_ref.shape[1]
    scales = read_scales(slots, rows, blocks, gathered_ref)
    for slot in range(slots):
        out_ref[slot] = kernel_product(slot, slots, rows, blocks, gathered_ref, kernel_ref, scales)


def last_kernel(
    slots, waves, radial_count,
    place_ref, held_ref, first_ref, counts_ref, field_ref, psi_ref, half_ref, term_ref, below_ref, above_ref,
    out_ref,
):
    rows, lanes = psi_ref.shape[1:]
    held, first = held_ref[0], first_ref[0]
    momenta = momenta_of(place_ref[1], rows, radial_count)
    lowest, highest = below_ref[...].astype(jnp.float32), above_ref[...].astype(jnp.float32)
    for slot in range(slots):
        below = lowest if slot == 0 else half_ref[slot - 1]
        above = highest if slot == slots - 1 else jnp.where(slot + 1 < held, half_ref[slot + 1], highest)
        flow, keep = derivative(
            slot, first, held, waves, counts_ref, field_ref[1, 0], field_ref[1, 1], momenta,
            half_ref[slot], term_ref[slot], below, above,
        )
        out_ref[slot] = jnp.where(keep, psi_ref[slot] + step_length * flow, 0.0)


def shards(al_count, ka_count, amplitudes, kernel, block_lengths, m_counts, vector_potential):
    slots, rows, lanes = amplitudes.shape
    radial_count = kernel.shape[2]
    waves = m_counts.shape[0]
    sent_rows = slots * rows + 16
    smem = pl.BlockSpec(memory_space=pltpu.SMEM)
    vmem = pl.BlockSpec(memory_space=pltpu.VMEM)
    params = pltpu.CompilerParams(vmem_limit_bytes=VMEM_LIMIT)
    f32, bf16 = jnp.float32, jnp.bfloat16
    shape = jax.ShapeDtypeStruct
    edge = shape((rows, lanes), bf16)
    sent = shape((sent_rows, lanes), bf16)
    state = shape((slots, rows, lanes), f32)
    place = jnp.stack([lax.axis_index("al"), lax.axis_index("ka")]).astype(jnp.int32)

    route = []
    for d in range(al_count):
        for k in range(1, ka_count):
            source = d - k if 2 * d < al_count else d + k
            if 0 <= source < al_count:
                route.append((source * ka_count + k, d * ka_count + k))
    other = lax.ppermute(block_lengths, ("al", "ka"), route)
    upward = [(i, i + 1) for i in range(al_count - 1)]
    downward = [(i + 1, i) for i in range(al_count - 1)]

    def exchange(low, high):
        return lax.ppermute(high, "al", upward), lax.ppermute(low, "al", downward)

    def gather(payload):
        payload = lax.optimization_barrier(payload.astype(jnp.float16))
        everything = lax.optimization_barrier(lax.all_gather(payload, "ka", axis=0, tiled=False))
        return everything.astype(bf16)

    encoded, low, high = pl.pallas_call(
        functools.partial(encode_kernel, slots),
        out_shape=(sent, edge, edge),
        in_specs=[smem, vmem],
        out_specs=(vmem, vmem, vmem),
        compiler_params=params,
        name="encode",
    )(block_lengths, amplitudes)
    below, above = exchange(low, high)
    row = lax.broadcasted_iota(jnp.int32, (sent_rows, lanes), 0)
    encoded = jnp.where(row >= sent_rows - 8, other[0].astype(f32).astype(bf16), encoded)
    gathered = gather(encoded)
    half, encoded, low, high, first = pl.pallas_call(
        functools.partial(half_kernel, slots, waves, ka_count, al_count),
        out_shape=(state, sent, edge, edge, shape((1,), jnp.int32)),
        in_specs=[smem] * 4 + [vmem] * 5,
        out_specs=(vmem, vmem, vmem, vmem, smem),
        compiler_params=params,
        name="half",
    )(place, block_lengths, m_counts, vector_potential, amplitudes, gathered, kernel, below, above)
    gathered = gather(encoded)
    below, above = exchange(low, high)
    term = pl.pallas_call(
        functools.partial(product_kernel, slots, ka_count),
        out_shape=state,
        in_specs=[vmem] * 2,
        out_specs=vmem,
        compiler_params=params,
        cost_estimate=pl.CostEstimate(
            flops=2 * slots * rows * radial_count * lanes * 8, bytes_accessed=4 * 1024 * 1024, transcendentals=0
        ),
        name="product",
    )(gathered, kernel)
    return pl.pallas_call(
        functools.partial(last_kernel, slots, waves, radial_count),
        out_shape=state,
        in_specs=[smem] * 5 + [vmem] * 5,
        out_specs=vmem,
        compiler_params=params,
        name="last",
    )(place, block_lengths, first, m_counts, vector_potential, amplitudes, half, term, below, above)


def solution(mesh):
    in_specs = (P("al", "ka", None), P("al", "ka", None), P("al"), P(), P())
    out_specs = P("al", "ka", None)
    body = functools.partial(shards, mesh.shape["al"], mesh.shape["ka"])
    return jax.shard_map(body, mesh=mesh, in_specs=in_specs, out_specs=out_specs, check_vma=False)
```

```python
import functools

import jax
import jax.numpy as jnp
from jax import lax
from jax.experimental import pallas as pl
from jax.experimental.pallas import tpu as pltpu
from jax.sharding import PartitionSpec as P

step_length = 0.2
momentum_top = 3.0
TOP = 13
VMEM_LIMIT = 32 * 1024 * 1024


def encode(rounded, out_ref, slot):
    rows = rounded.shape[0]
    values = rounded.astype(jnp.float32)
    largest = jnp.max(jnp.abs(values), axis=0, keepdims=True)
    exponent = jnp.clip(jnp.floor(jnp.log2(jnp.maximum(largest, 1e-36))), -110.0, 127.0)
    scaled = values * jnp.exp2(TOP - exponent)
    out_ref[slot * rows : (slot + 1) * rows, :] = scaled.astype(out_ref.dtype)
    return exponent


def store_exponents(exponents, out_ref, start):
    lanes = exponents[0].shape[1]
    pad = out_ref.shape[0] - start - len(exponents)
    rows = jnp.concatenate(exponents + [jnp.zeros((pad, lanes), jnp.float32)], axis=0)
    out_ref[start:, :] = rows.astype(out_ref.dtype)


def encode_kernel(slots, length_ref, psi_in, out_ref, low_ref, high_ref, psi_ref, held_ref):
    rows = psi_ref.shape[1]
    held_ref[...] = jnp.full(held_ref.shape, length_ref[0].astype(jnp.float32)).astype(held_ref.dtype)
    exponents = []
    for slot in range(slots):
        psi_ref[slot] = psi_in[slot]
        rounded = psi_in[slot].astype(jnp.bfloat16)
        exponents.append(encode(rounded, out_ref, slot))
    store_exponents(exponents, out_ref, slots * rows)
    low_ref[...] = psi_in[0].astype(jnp.bfloat16)
    high_ref[...] = psi_in[length_ref[0] - 1].astype(jnp.bfloat16)


def insert_kernel(encoded_ref, other_ref, kernel_in, out_ref, kernel_out):
    count = encoded_ref.shape[0] - 16
    tail = encoded_ref[count:, :].astype(jnp.float32)
    row = lax.broadcasted_iota(jnp.int32, tail.shape, 0)
    tail = jnp.where(row >= 8, other_ref[0:1].astype(jnp.float32), tail)
    out_ref[count:, :] = tail.astype(out_ref.dtype)


def kernel_product(slot, rows, blocks, gathered_ref, kernel_ref, scales):
    total = None
    for pair in range(0, blocks, 2):
        pieces = []
        for block in (pair, pair + 1):
            piece = gathered_ref[block, slot * rows : (slot + 1) * rows, :]
            scale = scales[block][slot : slot + 1]
            pieces.append((piece.astype(jnp.float32) * scale).astype(jnp.bfloat16))
        part = jnp.dot(
            kernel_ref[slot, :, pair * rows : (pair + 2) * rows],
            jnp.concatenate(pieces, axis=0),
            preferred_element_type=jnp.float32,
        )
        total = part if total is None else total + part
    return total


def read_scales(start, blocks, gathered_ref):
    return [
        jnp.exp2(gathered_ref[b, start : start + 16, :].astype(jnp.float32) - TOP)
        for b in range(blocks)
    ]


def scalar(row):
    return jnp.max(row).astype(jnp.int32)


def coupling_factors(slots, waves, first, counts, lanes):
    shape = (4 * slots, lanes)
    row = lax.broadcasted_iota(jnp.int32, shape, 0)
    lane = lax.broadcasted_iota(jnp.int32, shape, 1)
    slot, kind = row >> 2, row & 3
    q = jnp.where(lane < lanes // 2, lane, lane - lanes // 2)

    def pick(offset):
        value = jnp.full(shape, counts[offset], jnp.int32)
        for s in range(1, slots):
            value = jnp.where(slot == s, counts[s + offset], value)
        return value

    is_low = (kind & 1) == 0
    is_up = kind < 2
    count = pick(1)
    source = jnp.where(is_low, pick(0), pick(2))
    wave = first + slot
    other = wave + jnp.where(is_low, -1, 1)
    present = (other >= 0) & (other < waves)
    center = (count - 1) >> 1
    p = q + ((source - 1) >> 1) - center - jnp.where(is_up, 1, -1)
    allowed = (q < count) & (p >= 0) & (p < source) & present
    n = (q - center - jnp.where(is_up, 1, 0)).astype(jnp.float32)
    v = (wave + jnp.where(is_up, jnp.where(is_low, -1, 1), 0)).astype(jnp.float32)
    rises = (kind == 0) | (kind == 3)
    top = jnp.where(rises, (v + n + 1.0) * (v + n + 2.0), (v - n) * (v - n - 1.0))
    bottom = (2.0 * v + 1.0) * jnp.where(rises, 2.0 * v + 3.0, 2.0 * v - 1.0)
    size = jnp.sqrt(jnp.maximum(top, 0.0) / jnp.maximum(bottom, 1.0))
    return jnp.where(allowed, jnp.where(rises, size, -size), 0.0)


def lane_masks(slots, held, counts, lanes):
    lane = lax.broadcasted_iota(jnp.int32, (1, lanes), 1)
    q = jnp.where(lane < lanes // 2, lane, lane - lanes // 2)
    return [(q < counts[s + 1]) & (s < held) for s in range(slots)]


def coupled(slot, slots, held, counts, factors, states, lowest, highest):
    lanes = lowest.shape[1]
    below = lowest if slot == 0 else states[slot - 1]
    above = highest if slot == slots - 1 else jnp.where(slot + 1 < held, states[slot + 1], highest)
    center = (counts[slot + 1] - 1) >> 1
    sums = []
    for change, kind in ((1, 0), (-1, 2)):
        total = None
        for source, offset in ((below, 0), (above, 1)):
            shift = ((counts[slot + 2 * offset] - 1) >> 1) - center - change
            turned = pltpu.roll(source, (2 * lanes - shift) & (lanes - 1), 1)
            row = 4 * slot + kind + offset
            term = factors[row : row + 1] * turned
            total = term if total is None else total + term
        sums.append(total)
    return sums


def flow_of(current, term, up, down, field_x, field_y, momenta, kinetic):
    lanes = current.shape[1]
    lane = lax.broadcasted_iota(jnp.int32, (1, lanes), 1)
    turn = kinetic * current + term + momenta * (field_x * (up + down))
    swapped = pltpu.roll(turn, lanes // 2, 1)
    swapped = jnp.where(lane < lanes // 2, swapped, -swapped)
    return swapped + momenta * (field_y * (down - up))


def momenta_of(rows, lanes, radial_count):
    row = lax.broadcasted_iota(jnp.int32, (rows, lanes), 0) + lax.axis_index("ka") * rows
    momenta = (row.astype(jnp.float32) + 0.5) * (momentum_top / radial_count)
    return momenta, 0.5 * (momenta * momenta)


def half_kernel(
    slots, waves, blocks, al_count,
    held_ref, counts_ref, field_ref, psi_ref, gathered_ref, below_ref, above_ref, kernel_ref,
    half_ref, out_ref, low_ref, high_ref, factor_ref,
):
    rows, lanes = psi_ref.shape[1:]
    start = slots * rows
    seen = None
    for block in range(blocks):
        row = gathered_ref[block, start : start + 16, :].astype(jnp.float32)[8:9]
        seen = row if seen is None else seen + row
    seen = scalar(seen)
    held = scalar(held_ref[0:1].astype(jnp.float32))
    first = jnp.where(2 * lax.axis_index("al") < al_count, seen, waves - held - seen)
    lane = lax.broadcasted_iota(jnp.int32, (1, lanes), 1)
    known = jnp.concatenate(
        [counts_ref[...].astype(jnp.float32), jnp.zeros((1, lanes - waves), jnp.float32)], axis=1
    )
    counts = [
        scalar(jnp.where(lane == jnp.clip(first - 1 + i, 0, waves - 1), known, 0.0))
        for i in range(slots + 2)
    ]
    factors = coupling_factors(slots, waves, first, counts, lanes)
    notes = jnp.full((16, lanes), held.astype(jnp.float32))
    line = lax.broadcasted_iota(jnp.int32, (16, lanes), 0)
    for i in range(slots + 2):
        notes = jnp.where(line == i, counts[i].astype(jnp.float32), notes)
    halves = [
        jnp.broadcast_to(0.5 * field_ref[section : section + 1, part : part + 1], (1, lanes))
        for section in range(2)
        for part in range(2)
    ]
    for i in range(2):
        notes = jnp.where(line == 8 + i, halves[2 + i], notes)
    factor_ref[...] = jnp.concatenate([factors, notes], axis=0)
    masks = lane_masks(slots, held, counts, lanes)
    momenta, kinetic = momenta_of(rows, lanes, kernel_ref.shape[2])
    scales = read_scales(start, blocks, gathered_ref)
    psi = [jnp.where(masks[s], psi_ref[s], 0.0) for s in range(slots)]
    lowest, highest = below_ref[...].astype(jnp.float32), above_ref[...].astype(jnp.float32)
    exponents = []
    for slot in range(slots):
        up, down = coupled(slot, slots, held, counts, factors, psi, lowest, highest)
        term = kernel_product(slot, rows, blocks, gathered_ref, kernel_ref, scales)
        flow = flow_of(psi[slot], term, up, down, halves[0], halves[1], momenta, kinetic)
        half = jnp.where(masks[slot], psi[slot] + (0.5 * step_length) * flow, 0.0)
        half_ref[slot] = half
        rounded = half.astype(jnp.bfloat16)
        exponents.append(encode(rounded, out_ref, slot))
        if slot == 0:
            low_ref[...] = rounded

        @pl.when(slot == held - 1)
        def _():
            high_ref[...] = rounded

    store_exponents(exponents, out_ref, start)


def product_kernel(slots, blocks, gathered_ref, kernel_ref, out_ref):
    rows = out_ref.shape[1]
    scales = read_scales(slots * rows, blocks, gathered_ref)
    for slot in range(slots):
        out_ref[slot] = kernel_product(slot, rows, blocks, gathered_ref, kernel_ref, scales)


def last_kernel(
    slots, radial_count, factor_ref, psi_ref, half_ref, term_ref, below_ref, above_ref,
    out_hbm, out_ref, sems,
):
    rows, lanes = psi_ref.shape[1:]
    base = 4 * slots
    counts = [scalar(factor_ref[base + i : base + i + 1]) for i in range(slots + 2)]
    held = scalar(factor_ref[base + slots + 2 : base + slots + 3])
    factors = factor_ref[0:base]
    fields = factor_ref[base + 8 : base + 9], factor_ref[base + 9 : base + 10]
    masks = lane_masks(slots, held, counts, lanes)
    momenta, kinetic = momenta_of(rows, lanes, radial_count)
    lowest, highest = below_ref[...].astype(jnp.float32), above_ref[...].astype(jnp.float32)
    states = [half_ref[s] for s in range(slots)]
    copies = []
    for slot in range(slots):
        up, down = coupled(slot, slots, held, counts, factors, states, lowest, highest)
        flow = flow_of(states[slot], term_ref[slot], up, down, *fields, momenta, kinetic)
        out_ref[slot] = jnp.where(masks[slot], psi_ref[slot] + step_length * flow, 0.0)
        copies.append(pltpu.make_async_copy(out_ref.at[slot], out_hbm.at[slot], sems.at[slot]))
        copies[slot].start()
    for copy in copies:
        copy.wait()


def shards(al_count, ka_count, amplitudes, kernel, block_lengths, m_counts, vector_potential):
    slots, rows, lanes = amplitudes.shape
    radial_count = kernel.shape[2]
    waves = m_counts.shape[0]
    sent_rows = slots * rows + 16
    vmem = pl.BlockSpec(memory_space=pltpu.VMEM)
    hbm = pl.BlockSpec(memory_space=pltpu.HBM)
    params = pltpu.CompilerParams(vmem_limit_bytes=VMEM_LIMIT)
    f32, bf16 = jnp.float32, jnp.bfloat16
    shape = jax.ShapeDtypeStruct
    edge = shape((rows, lanes), bf16)
    sent = shape((sent_rows, lanes), bf16)
    state = shape((slots, rows, lanes), f32)
    sems = pltpu.SemaphoreType.DMA((slots,))

    route = []
    for d in range(al_count):
        for k in range(1, ka_count):
            source = d - k if 2 * d < al_count else d + k
            if 0 <= source < al_count:
                route.append((source * ka_count + k, d * ka_count + k))
    upward = [(i, i + 1) for i in range(al_count - 1)]
    downward = [(i + 1, i) for i in range(al_count - 1)]

    def exchange(low, high):
        return lax.ppermute(high, "al", upward), lax.ppermute(low, "al", downward)

    def gather(payload):
        payload = lax.optimization_barrier(payload.astype(jnp.float16))
        everything = lax.optimization_barrier(lax.all_gather(payload, "ka", axis=0, tiled=False))
        return everything.astype(bf16)

    encoded, low, high, psi, held = pl.pallas_call(
        functools.partial(encode_kernel, slots),
        out_shape=(sent, edge, edge, state, shape((16, lanes), bf16)),
        in_specs=[pl.BlockSpec(memory_space=pltpu.SMEM), vmem],
        out_specs=(vmem,) * 5,
        compiler_params=params,
        name="encode",
    )(block_lengths, amplitudes)
    other = lax.ppermute(held, ("al", "ka"), route)
    below, above = exchange(low, high)
    encoded, kernel = pl.pallas_call(
        insert_kernel,
        out_shape=(sent, shape(kernel.shape, bf16)),
        in_specs=[vmem] * 3,
        out_specs=(vmem,) * 2,
        input_output_aliases={0: 0, 2: 1},
        compiler_params=params,
        name="insert",
    )(encoded, other, kernel)
    gathered = gather(encoded)
    half, encoded, low, high, factors = pl.pallas_call(
        functools.partial(half_kernel, slots, waves, ka_count, al_count),
        out_shape=(state, sent, edge, edge, shape((4 * slots + 16, lanes), f32)),
        in_specs=[vmem] * 8,
        out_specs=(vmem,) * 5,
        compiler_params=params,
        name="half",
    )(held, m_counts[None], vector_potential, psi, gathered, below, above, kernel)
    gathered = gather(encoded)
    below, above = exchange(low, high)
    term = pl.pallas_call(
        functools.partial(product_kernel, slots, ka_count),
        out_shape=state,
        in_specs=[vmem] * 2,
        out_specs=vmem,
        compiler_params=params,
        cost_estimate=pl.CostEstimate(
            flops=2 * slots * rows * radial_count * lanes * 8, bytes_accessed=4 * 1024 * 1024, transcendentals=0
        ),
        name="product",
    )(gathered, kernel)
    return pl.pallas_call(
        functools.partial(last_kernel, slots, radial_count),
        out_shape=state,
        in_specs=[vmem] * 6,
        out_specs=hbm,
        scratch_shapes=[pltpu.VMEM((slots, rows, lanes), f32), sems],
        compiler_params=params,
        name="last",
    )(factors, psi, half, term, below, above)


def solution(mesh):
    in_specs = (P("al", "ka", None), P("al", "ka", None), P("al"), P(), P())
    out_specs = P("al", "ka", None)
    body = functools.partial(shards, mesh.shape["al"], mesh.shape["ka"])
    return jax.shard_map(body, mesh=mesh, in_specs=in_specs, out_specs=out_specs, check_vma=False)
```

```python
import functools

import jax
import jax.numpy as jnp
from jax import lax
from jax.experimental import pallas as pl
from jax.experimental.pallas import tpu as pltpu
from jax.sharding import PartitionSpec as P

step_length = 0.2
momentum_top = 3.0
TOP = 13
VMEM_LIMIT = 32 * 1024 * 1024


def encode(rounded, out_ref, slot):
    rows = rounded.shape[0]
    values = rounded.astype(jnp.float32)
    largest = jnp.max(jnp.abs(values), axis=0, keepdims=True)
    exponent = jnp.clip(jnp.floor(jnp.log2(jnp.maximum(largest, 1e-36))), -110.0, 127.0)
    scaled = values * jnp.exp2(TOP - exponent)
    out_ref[slot * rows : (slot + 1) * rows, :] = scaled.astype(out_ref.dtype)
    return exponent


def store_exponents(exponents, out_ref, start):
    lanes = exponents[0].shape[1]
    pad = out_ref.shape[0] - start - len(exponents)
    rows = jnp.concatenate(exponents + [jnp.zeros((pad, lanes), jnp.float32)], axis=0)
    out_ref[start:, :] = rows.astype(out_ref.dtype)


def is_even():
    return (lax.axis_index("al") & 1) == 0


def edges_of(first_ref, second_ref):
    first, second = first_ref[...].astype(jnp.float32), second_ref[...].astype(jnp.float32)
    even = is_even()
    return jnp.where(even, second, first), jnp.where(even, first, second)


def encode_kernel(slots, length_ref, psi_in, out_ref, next_ref, other_ref, psi_ref, held_ref):
    rows = psi_ref.shape[1]
    held_ref[...] = jnp.full(held_ref.shape, length_ref[0].astype(jnp.float32)).astype(held_ref.dtype)
    exponents = []
    for slot in range(slots):
        psi_ref[slot] = psi_in[slot]
        rounded = psi_in[slot].astype(jnp.bfloat16)
        exponents.append(encode(rounded, out_ref, slot))
    store_exponents(exponents, out_ref, slots * rows)
    high = length_ref[0] - 1
    even = is_even()
    next_ref[...] = psi_in[jnp.where(even, high, 0)].astype(jnp.bfloat16)
    other_ref[...] = psi_in[jnp.where(even, 0, high)].astype(jnp.bfloat16)


def insert_kernel(encoded_ref, other_ref, kernel_in, out_ref, kernel_out):
    count = encoded_ref.shape[0] - 16
    tail = encoded_ref[count:, :].astype(jnp.float32)
    row = lax.broadcasted_iota(jnp.int32, tail.shape, 0)
    tail = jnp.where(row >= 8, other_ref[0:1].astype(jnp.float32), tail)
    out_ref[count:, :] = tail.astype(out_ref.dtype)


def kernel_product(slot, rows, blocks, gathered_ref, kernel_ref, scales):
    total = None
    for pair in range(0, blocks, 2):
        pieces = []
        for block in (pair, pair + 1):
            piece = gathered_ref[block, slot * rows : (slot + 1) * rows, :]
            scale = scales[block][slot : slot + 1]
            pieces.append((piece.astype(jnp.float32) * scale).astype(jnp.bfloat16))
        part = jnp.dot(
            kernel_ref[slot, :, pair * rows : (pair + 2) * rows],
            jnp.concatenate(pieces, axis=0),
            preferred_element_type=jnp.float32,
        )
        total = part if total is None else total + part
    return total


def read_scales(start, blocks, gathered_ref):
    return [
        jnp.exp2(gathered_ref[b, start : start + 16, :].astype(jnp.float32) - TOP)
        for b in range(blocks)
    ]


def scalar(row):
    return jnp.max(row).astype(jnp.int32)


def coupling_factors(slots, waves, first, counts, lanes):
    shape = (4 * slots, lanes)
    row = lax.broadcasted_iota(jnp.int32, shape, 0)
    lane = lax.broadcasted_iota(jnp.int32, shape, 1)
    slot, kind = row >> 2, row & 3
    q = jnp.where(lane < lanes // 2, lane, lane - lanes // 2)

    def pick(offset):
        value = jnp.full(shape, counts[offset], jnp.int32)
        for s in range(1, slots):
            value = jnp.where(slot == s, counts[s + offset], value)
        return value

    is_low = (kind & 1) == 0
    is_up = kind < 2
    count = pick(1)
    source = jnp.where(is_low, pick(0), pick(2))
    wave = first + slot
    other = wave + jnp.where(is_low, -1, 1)
    present = (other >= 0) & (other < waves)
    center = (count - 1) >> 1
    p = q + ((source - 1) >> 1) - center - jnp.where(is_up, 1, -1)
    allowed = (q < count) & (p >= 0) & (p < source) & present
    n = (q - center - jnp.where(is_up, 1, 0)).astype(jnp.float32)
    v = (wave + jnp.where(is_up, jnp.where(is_low, -1, 1), 0)).astype(jnp.float32)
    rises = (kind == 0) | (kind == 3)
    top = jnp.where(rises, (v + n + 1.0) * (v + n + 2.0), (v - n) * (v - n - 1.0))
    bottom = (2.0 * v + 1.0) * jnp.where(rises, 2.0 * v + 3.0, 2.0 * v - 1.0)
    size = jnp.sqrt(jnp.maximum(top, 0.0) / jnp.maximum(bottom, 1.0))
    return jnp.where(allowed, jnp.where(rises, size, -size), 0.0)


def lane_masks(slots, held, counts, lanes):
    lane = lax.broadcasted_iota(jnp.int32, (1, lanes), 1)
    q = jnp.where(lane < lanes // 2, lane, lane - lanes // 2)
    return [(q < counts[s + 1]) & (s < held) for s in range(slots)]


def coupled(slot, slots, held, counts, factors, states, lowest, highest):
    lanes = lowest.shape[1]
    below = lowest if slot == 0 else states[slot - 1]
    above = highest if slot == slots - 1 else jnp.where(slot + 1 < held, states[slot + 1], highest)
    center = (counts[slot + 1] - 1) >> 1
    sums = []
    for change, kind in ((1, 0), (-1, 2)):
        total = None
        for source, offset in ((below, 0), (above, 1)):
            shift = ((counts[slot + 2 * offset] - 1) >> 1) - center - change
            turned = pltpu.roll(source, (2 * lanes - shift) & (lanes - 1), 1)
            row = 4 * slot + kind + offset
            term = factors[row : row + 1] * turned
            total = term if total is None else total + term
        sums.append(total)
    return sums


def flow_of(current, term, up, down, field_x, field_y, momenta, kinetic):
    lanes = current.shape[1]
    lane = lax.broadcasted_iota(jnp.int32, (1, lanes), 1)
    turn = kinetic * current + term + momenta * (field_x * (up + down))
    swapped = pltpu.roll(turn, lanes // 2, 1)
    swapped = jnp.where(lane < lanes // 2, swapped, -swapped)
    return swapped + momenta * (field_y * (down - up))


def momenta_of(rows, lanes, radial_count):
    row = lax.broadcasted_iota(jnp.int32, (rows, lanes), 0) + lax.axis_index("ka") * rows
    momenta = (row.astype(jnp.float32) + 0.5) * (momentum_top / radial_count)
    return momenta, 0.5 * (momenta * momenta)


def half_kernel(
    slots, waves, blocks, al_count,
    held_ref, counts_ref, field_ref, psi_ref, gathered_ref, first_ref, second_ref, kernel_ref,
    half_ref, out_ref, next_ref, other_ref, factor_ref,
):
    rows, lanes = psi_ref.shape[1:]
    start = slots * rows
    seen = None
    for block in range(blocks):
        row = gathered_ref[block, start : start + 16, :].astype(jnp.float32)[8:9]
        seen = row if seen is None else seen + row
    seen = scalar(seen)
    held = scalar(held_ref[0:1].astype(jnp.float32))
    first = jnp.where(2 * lax.axis_index("al") < al_count, seen, waves - held - seen)
    lane = lax.broadcasted_iota(jnp.int32, (1, lanes), 1)
    known = jnp.concatenate(
        [counts_ref[...].astype(jnp.float32), jnp.zeros((1, lanes - waves), jnp.float32)], axis=1
    )
    counts = [
        scalar(jnp.where(lane == jnp.clip(first - 1 + i, 0, waves - 1), known, 0.0))
        for i in range(slots + 2)
    ]
    factors = coupling_factors(slots, waves, first, counts, lanes)
    notes = jnp.full((16, lanes), held.astype(jnp.float32))
    line = lax.broadcasted_iota(jnp.int32, (16, lanes), 0)
    for i in range(slots + 2):
        notes = jnp.where(line == i, counts[i].astype(jnp.float32), notes)
    halves = [
        jnp.broadcast_to(0.5 * field_ref[section : section + 1, part : part + 1], (1, lanes))
        for section in range(2)
        for part in range(2)
    ]
    for i in range(2):
        notes = jnp.where(line == 8 + i, halves[2 + i], notes)
    factor_ref[...] = jnp.concatenate([factors, notes], axis=0)
    masks = lane_masks(slots, held, counts, lanes)
    momenta, kinetic = momenta_of(rows, lanes, kernel_ref.shape[2])
    scales = read_scales(start, blocks, gathered_ref)
    psi = [jnp.where(masks[s], psi_ref[s], 0.0) for s in range(slots)]
    lowest, highest = edges_of(first_ref, second_ref)
    exponents = []
    for slot in range(slots):
        up, down = coupled(slot, slots, held, counts, factors, psi, lowest, highest)
        term = kernel_product(slot, rows, blocks, gathered_ref, kernel_ref, scales)
        flow = flow_of(psi[slot], term, up, down, halves[0], halves[1], momenta, kinetic)
        half = jnp.where(masks[slot], psi[slot] + (0.5 * step_length) * flow, 0.0)
        half_ref[slot] = half
        rounded = half.astype(jnp.bfloat16)
        exponents.append(encode(rounded, out_ref, slot))
    store_exponents(exponents, out_ref, start)
    even = is_even()
    next_ref[...] = half_ref[jnp.where(even, held - 1, 0)].astype(jnp.bfloat16)
    other_ref[...] = half_ref[jnp.where(even, 0, held - 1)].astype(jnp.bfloat16)


def product_kernel(slots, blocks, gathered_ref, kernel_ref, out_ref):
    rows = out_ref.shape[1]
    scales = read_scales(slots * rows, blocks, gathered_ref)
    for slot in range(slots):
        out_ref[slot] = kernel_product(slot, rows, blocks, gathered_ref, kernel_ref, scales)


def last_kernel(
    slots, radial_count, factor_ref, psi_ref, half_ref, term_ref, first_ref, second_ref,
    out_hbm, out_ref, sems,
):
    rows, lanes = psi_ref.shape[1:]
    base = 4 * slots
    counts = [scalar(factor_ref[base + i : base + i + 1]) for i in range(slots + 2)]
    held = scalar(factor_ref[base + slots + 2 : base + slots + 3])
    factors = factor_ref[0:base]
    fields = factor_ref[base + 8 : base + 9], factor_ref[base + 9 : base + 10]
    masks = lane_masks(slots, held, counts, lanes)
    momenta, kinetic = momenta_of(rows, lanes, radial_count)
    lowest, highest = edges_of(first_ref, second_ref)
    states = [half_ref[s] for s in range(slots)]
    copies = []
    for slot in range(slots):
        up, down = coupled(slot, slots, held, counts, factors, states, lowest, highest)
        flow = flow_of(states[slot], term_ref[slot], up, down, *fields, momenta, kinetic)
        out_ref[slot] = jnp.where(masks[slot], psi_ref[slot] + step_length * flow, 0.0)
        copies.append(pltpu.make_async_copy(out_ref.at[slot], out_hbm.at[slot], sems.at[slot]))
        copies[slot].start()
    for copy in copies:
        copy.wait()


def shards(al_count, ka_count, amplitudes, kernel, block_lengths, m_counts, vector_potential):
    slots, rows, lanes = amplitudes.shape
    radial_count = kernel.shape[2]
    waves = m_counts.shape[0]
    sent_rows = slots * rows + 16
    vmem = pl.BlockSpec(memory_space=pltpu.VMEM)
    hbm = pl.BlockSpec(memory_space=pltpu.HBM)
    params = pltpu.CompilerParams(vmem_limit_bytes=VMEM_LIMIT)
    f32, bf16 = jnp.float32, jnp.bfloat16
    shape = jax.ShapeDtypeStruct
    edge = shape((rows, lanes), bf16)
    sent = shape((sent_rows, lanes), bf16)
    state = shape((slots, rows, lanes), f32)
    sems = pltpu.SemaphoreType.DMA((slots,))

    route = []
    for target in range(al_count // 2):
        for source in range(target):
            route.append((source * ka_count + target, target * ka_count + source))
            source_twin, target_twin = al_count - 1 - source, al_count - 1 - target
            route.append((source_twin * ka_count + target, target_twin * ka_count + source))
    def pairs(start):
        return [(i + a, i + 1 - a) for i in range(start, al_count - 1, 2) for a in (0, 1)]

    def exchange(following, other):
        return lax.ppermute(following, "al", pairs(0)), lax.ppermute(other, "al", pairs(1))

    def gather(payload):
        payload = lax.optimization_barrier(payload.astype(jnp.float16))
        everything = lax.optimization_barrier(lax.all_gather(payload, "ka", axis=0, tiled=False))
        return everything.astype(bf16)

    encoded, following, other_edge, psi, held = pl.pallas_call(
        functools.partial(encode_kernel, slots),
        out_shape=(sent, edge, edge, state, shape((16, lanes), bf16)),
        in_specs=[pl.BlockSpec(memory_space=pltpu.SMEM), vmem],
        out_specs=(vmem,) * 5,
        compiler_params=params,
        name="encode",
    )(block_lengths, amplitudes)
    other = lax.ppermute(held, ("al", "ka"), route)
    first_edge, second_edge = exchange(following, other_edge)
    encoded, kernel = pl.pallas_call(
        insert_kernel,
        out_shape=(sent, shape(kernel.shape, bf16)),
        in_specs=[vmem] * 3,
        out_specs=(vmem,) * 2,
        input_output_aliases={0: 0, 2: 1},
        compiler_params=params,
        name="insert",
    )(encoded, other, kernel)
    gathered = gather(encoded)
    half, encoded, following, other_edge, factors = pl.pallas_call(
        functools.partial(half_kernel, slots, waves, ka_count, al_count),
        out_shape=(state, sent, edge, edge, shape((4 * slots + 16, lanes), f32)),
        in_specs=[vmem] * 8,
        out_specs=(vmem,) * 5,
        compiler_params=params,
        name="half",
    )(held, m_counts[None], vector_potential, psi, gathered, first_edge, second_edge, kernel)
    gathered = gather(encoded)
    first_edge, second_edge = exchange(following, other_edge)
    term = pl.pallas_call(
        functools.partial(product_kernel, slots, ka_count),
        out_shape=state,
        in_specs=[vmem] * 2,
        out_specs=vmem,
        compiler_params=params,
        cost_estimate=pl.CostEstimate(
            flops=2 * slots * rows * radial_count * lanes * 8, bytes_accessed=4 * 1024 * 1024, transcendentals=0
        ),
        name="product",
    )(gathered, kernel)
    return pl.pallas_call(
        functools.partial(last_kernel, slots, radial_count),
        out_shape=state,
        in_specs=[vmem] * 6,
        out_specs=hbm,
        scratch_shapes=[pltpu.VMEM((slots, rows, lanes), f32), sems],
        compiler_params=params,
        name="last",
    )(factors, psi, half, term, first_edge, second_edge)


def solution(mesh):
    in_specs = (P("al", "ka", None), P("al", "ka", None), P("al"), P(), P())
    out_specs = P("al", "ka", None)
    body = functools.partial(shards, mesh.shape["al"], mesh.shape["ka"])
    return jax.shard_map(body, mesh=mesh, in_specs=in_specs, out_specs=out_specs, check_vma=False)
```

```python
import functools

import jax
import jax.numpy as jnp
from jax import lax
from jax.experimental import pallas as pl
from jax.experimental.pallas import tpu as pltpu
from jax.sharding import PartitionSpec as P

step_length = 0.2
momentum_top = 3.0
TOP = 13
VMEM_LIMIT = 32 * 1024 * 1024


def encode(rounded, out_ref, slot):
    rows = rounded.shape[0]
    values = rounded.astype(jnp.float32)
    largest = jnp.max(jnp.abs(values), axis=0, keepdims=True)
    exponent = jnp.clip(jnp.floor(jnp.log2(jnp.maximum(largest, 1e-36))), -110.0, 127.0)
    scaled = values * jnp.exp2(TOP - exponent)
    out_ref[slot * rows : (slot + 1) * rows, :] = scaled.astype(out_ref.dtype)
    return exponent


def store_exponents(exponents, out_ref, start):
    lanes = exponents[0].shape[1]
    pad = out_ref.shape[0] - start - len(exponents)
    rows = jnp.concatenate(exponents + [jnp.zeros((pad, lanes), jnp.float32)], axis=0)
    out_ref[start:, :] = rows.astype(out_ref.dtype)


def is_even():
    return (lax.axis_index("al") & 1) == 0


def edges_of(first_ref, second_ref):
    first, second = first_ref[...].astype(jnp.float32), second_ref[...].astype(jnp.float32)
    even = is_even()
    return jnp.where(even, second, first), jnp.where(even, first, second)


def encode_kernel(slots, length_ref, psi_in, out_ref, next_ref, other_ref, psi_ref, held_ref):
    rows = psi_ref.shape[1]
    length = scalar(length_ref[...].astype(jnp.float32))
    held_ref[...] = jnp.full(held_ref.shape, length.astype(jnp.float32)).astype(held_ref.dtype)
    exponents = []
    for slot in range(slots):
        psi_ref[slot] = psi_in[slot]
        rounded = psi_in[slot].astype(jnp.bfloat16)
        exponents.append(encode(rounded, out_ref, slot))
    store_exponents(exponents, out_ref, slots * rows)
    high = length - 1
    even = is_even()
    next_ref[...] = psi_in[jnp.where(even, high, 0)].astype(jnp.bfloat16)
    other_ref[...] = psi_in[jnp.where(even, 0, high)].astype(jnp.bfloat16)


def insert_kernel(encoded_ref, other_ref, kernel_in, out_ref, kernel_out):
    count = encoded_ref.shape[0] - 16
    tail = encoded_ref[count:, :].astype(jnp.float32)
    row = lax.broadcasted_iota(jnp.int32, tail.shape, 0)
    tail = jnp.where(row >= 8, other_ref[0:1].astype(jnp.float32), tail)
    out_ref[count:, :] = tail.astype(out_ref.dtype)


def kernel_product(slot, rows, blocks, gathered_ref, kernel_ref, scales):
    total = None
    for pair in range(0, blocks, 2):
        pieces = []
        for block in (pair, pair + 1):
            piece = gathered_ref[block, slot * rows : (slot + 1) * rows, :]
            scale = scales[block][slot : slot + 1]
            pieces.append((piece.astype(jnp.float32) * scale).astype(jnp.bfloat16))
        part = jnp.dot(
            kernel_ref[slot, :, pair * rows : (pair + 2) * rows],
            jnp.concatenate(pieces, axis=0),
            preferred_element_type=jnp.float32,
        )
        total = part if total is None else total + part
    return total


def read_scales(start, blocks, gathered_ref):
    return [
        jnp.exp2(gathered_ref[b, start : start + 16, :].astype(jnp.float32) - TOP)
        for b in range(blocks)
    ]


def scalar(row):
    return jnp.max(row).astype(jnp.int32)


def coupling_factors(slots, waves, first, counts, lanes):
    shape = (4 * slots, lanes)
    row = lax.broadcasted_iota(jnp.int32, shape, 0)
    lane = lax.broadcasted_iota(jnp.int32, shape, 1)
    slot, kind = row >> 2, row & 3
    q = jnp.where(lane < lanes // 2, lane, lane - lanes // 2)

    def pick(offset):
        value = jnp.full(shape, counts[offset], jnp.int32)
        for s in range(1, slots):
            value = jnp.where(slot == s, counts[s + offset], value)
        return value

    is_low = (kind & 1) == 0
    is_up = kind < 2
    count = pick(1)
    source = jnp.where(is_low, pick(0), pick(2))
    wave = first + slot
    other = wave + jnp.where(is_low, -1, 1)
    present = (other >= 0) & (other < waves)
    center = (count - 1) >> 1
    p = q + ((source - 1) >> 1) - center - jnp.where(is_up, 1, -1)
    allowed = (q < count) & (p >= 0) & (p < source) & present
    n = (q - center - jnp.where(is_up, 1, 0)).astype(jnp.float32)
    v = (wave + jnp.where(is_up, jnp.where(is_low, -1, 1), 0)).astype(jnp.float32)
    rises = (kind == 0) | (kind == 3)
    top = jnp.where(rises, (v + n + 1.0) * (v + n + 2.0), (v - n) * (v - n - 1.0))
    bottom = (2.0 * v + 1.0) * jnp.where(rises, 2.0 * v + 3.0, 2.0 * v - 1.0)
    size = jnp.sqrt(jnp.maximum(top, 0.0) / jnp.maximum(bottom, 1.0))
    return jnp.where(allowed, jnp.where(rises, size, -size), 0.0)


def lane_masks(slots, held, counts, lanes):
    lane = lax.broadcasted_iota(jnp.int32, (1, lanes), 1)
    q = jnp.where(lane < lanes // 2, lane, lane - lanes // 2)
    return [(q < counts[s + 1]) & (s < held) for s in range(slots)]


def coupled(slot, slots, held, counts, factors, states, lowest, highest):
    lanes = lowest.shape[1]
    below = lowest if slot == 0 else states[slot - 1]
    above = highest if slot == slots - 1 else jnp.where(slot + 1 < held, states[slot + 1], highest)
    center = (counts[slot + 1] - 1) >> 1
    sums = []
    for change, kind in ((1, 0), (-1, 2)):
        total = None
        for source, offset in ((below, 0), (above, 1)):
            shift = ((counts[slot + 2 * offset] - 1) >> 1) - center - change
            turned = pltpu.roll(source, (2 * lanes - shift) & (lanes - 1), 1)
            row = 4 * slot + kind + offset
            term = factors[row : row + 1] * turned
            total = term if total is None else total + term
        sums.append(total)
    return sums


def flow_of(current, term, up, down, field_x, field_y, momenta, kinetic):
    lanes = current.shape[1]
    lane = lax.broadcasted_iota(jnp.int32, (1, lanes), 1)
    turn = kinetic * current + term + momenta * (field_x * (up + down))
    swapped = pltpu.roll(turn, lanes // 2, 1)
    swapped = jnp.where(lane < lanes // 2, swapped, -swapped)
    return swapped + momenta * (field_y * (down - up))


def momenta_of(rows, lanes, radial_count):
    row = lax.broadcasted_iota(jnp.int32, (rows, lanes), 0) + lax.axis_index("ka") * rows
    momenta = (row.astype(jnp.float32) + 0.5) * (momentum_top / radial_count)
    return momenta, 0.5 * (momenta * momenta)


def half_kernel(
    slots, waves, blocks, al_count,
    held_ref, counts_ref, field_ref, psi_ref, gathered_ref, first_ref, second_ref, kernel_ref,
    half_ref, out_ref, next_ref, other_ref, factor_ref,
):
    rows, lanes = psi_ref.shape[1:]
    start = slots * rows
    seen = None
    for block in range(blocks):
        row = gathered_ref[block, start : start + 16, :].astype(jnp.float32)[8:9]
        seen = row if seen is None else seen + row
    seen = scalar(seen)
    held = scalar(held_ref[0:1].astype(jnp.float32))
    first = jnp.where(2 * lax.axis_index("al") < al_count, seen, waves - held - seen)
    lane = lax.broadcasted_iota(jnp.int32, (1, lanes), 1)
    known = jnp.concatenate(
        [counts_ref[...].astype(jnp.float32), jnp.zeros((1, lanes - waves), jnp.float32)], axis=1
    )
    counts = [
        scalar(jnp.where(lane == jnp.clip(first - 1 + i, 0, waves - 1), known, 0.0))
        for i in range(slots + 2)
    ]
    factors = coupling_factors(slots, waves, first, counts, lanes)
    notes = jnp.full((16, lanes), held.astype(jnp.float32))
    line = lax.broadcasted_iota(jnp.int32, (16, lanes), 0)
    for i in range(slots + 2):
        notes = jnp.where(line == i, counts[i].astype(jnp.float32), notes)
    halves = [
        jnp.broadcast_to(0.5 * field_ref[section : section + 1, part : part + 1], (1, lanes))
        for section in range(2)
        for part in range(2)
    ]
    for i in range(2):
        notes = jnp.where(line == 8 + i, halves[2 + i], notes)
    factor_ref[...] = jnp.concatenate([factors, notes], axis=0)
    masks = lane_masks(slots, held, counts, lanes)
    momenta, kinetic = momenta_of(rows, lanes, kernel_ref.shape[2])
    scales = read_scales(start, blocks, gathered_ref)
    psi = [jnp.where(masks[s], psi_ref[s], 0.0) for s in range(slots)]
    lowest, highest = edges_of(first_ref, second_ref)
    exponents = []
    for slot in range(slots):
        up, down = coupled(slot, slots, held, counts, factors, psi, lowest, highest)
        term = kernel_product(slot, rows, blocks, gathered_ref, kernel_ref, scales)
        flow = flow_of(psi[slot], term, up, down, halves[0], halves[1], momenta, kinetic)
        half = jnp.where(masks[slot], psi[slot] + (0.5 * step_length) * flow, 0.0)
        half_ref[slot] = half
        rounded = half.astype(jnp.bfloat16)
        exponents.append(encode(rounded, out_ref, slot))
    store_exponents(exponents, out_ref, start)
    even = is_even()
    next_ref[...] = half_ref[jnp.where(even, held - 1, 0)].astype(jnp.bfloat16)
    other_ref[...] = half_ref[jnp.where(even, 0, held - 1)].astype(jnp.bfloat16)


def product_kernel(slots, blocks, gathered_ref, kernel_ref, out_ref):
    rows = out_ref.shape[1]
    scales = read_scales(slots * rows, blocks, gathered_ref)
    for slot in range(slots):
        out_ref[slot] = kernel_product(slot, rows, blocks, gathered_ref, kernel_ref, scales)


def last_kernel(
    slots, radial_count, factor_ref, psi_ref, half_ref, term_ref, first_ref, second_ref,
    out_hbm, out_ref, sems,
):
    rows, lanes = psi_ref.shape[1:]
    base = 4 * slots
    counts = [scalar(factor_ref[base + i : base + i + 1]) for i in range(slots + 2)]
    held = scalar(factor_ref[base + slots + 2 : base + slots + 3])
    factors = factor_ref[0:base]
    fields = factor_ref[base + 8 : base + 9], factor_ref[base + 9 : base + 10]
    masks = lane_masks(slots, held, counts, lanes)
    momenta, kinetic = momenta_of(rows, lanes, radial_count)
    lowest, highest = edges_of(first_ref, second_ref)
    states = [half_ref[s] for s in range(slots)]
    copies = []
    for slot in range(slots):
        up, down = coupled(slot, slots, held, counts, factors, states, lowest, highest)
        flow = flow_of(states[slot], term_ref[slot], up, down, *fields, momenta, kinetic)
        out_ref[slot] = jnp.where(masks[slot], psi_ref[slot] + step_length * flow, 0.0)
        copies.append(pltpu.make_async_copy(out_ref.at[slot], out_hbm.at[slot], sems.at[slot]))
        copies[slot].start()
    for copy in copies:
        copy.wait()


def shards(al_count, ka_count, amplitudes, kernel, block_lengths, m_counts, vector_potential):
    slots, rows, lanes = amplitudes.shape
    radial_count = kernel.shape[2]
    waves = m_counts.shape[0]
    sent_rows = slots * rows + 16
    vmem = pl.BlockSpec(memory_space=pltpu.VMEM)
    hbm = pl.BlockSpec(memory_space=pltpu.HBM)
    params = pltpu.CompilerParams(vmem_limit_bytes=VMEM_LIMIT)
    f32, bf16 = jnp.float32, jnp.bfloat16
    shape = jax.ShapeDtypeStruct
    edge = shape((rows, lanes), bf16)
    sent = shape((sent_rows, lanes), bf16)
    state = shape((slots, rows, lanes), f32)
    sems = pltpu.SemaphoreType.DMA((slots,))

    route = []
    for target in range(al_count // 2):
        for source in range(target):
            route.append((source * ka_count + target, target * ka_count + source))
            source_twin, target_twin = al_count - 1 - source, al_count - 1 - target
            route.append((source_twin * ka_count + target, target_twin * ka_count + source))
    def pairs(start):
        return [(i + a, i + 1 - a) for i in range(start, al_count - 1, 2) for a in (0, 1)]

    def exchange(following, other):
        return lax.ppermute(following, "al", pairs(0)), lax.ppermute(other, "al", pairs(1))

    def gather(payload):
        payload = lax.optimization_barrier(payload.astype(jnp.float16))
        everything = lax.optimization_barrier(lax.all_gather(payload, "ka", axis=0, tiled=False))
        return everything.astype(bf16)

    encoded, following, other_edge, psi, held = pl.pallas_call(
        functools.partial(encode_kernel, slots),
        out_shape=(sent, edge, edge, state, shape((16, lanes), bf16)),
        in_specs=[vmem] * 2,
        out_specs=(vmem,) * 5,
        compiler_params=params,
        name="encode",
    )(block_lengths[None], amplitudes)
    other = lax.ppermute(held, ("al", "ka"), route)
    first_edge, second_edge = exchange(following, other_edge)
    encoded, kernel = pl.pallas_call(
        insert_kernel,
        out_shape=(sent, shape(kernel.shape, bf16)),
        in_specs=[vmem] * 3,
        out_specs=(vmem,) * 2,
        input_output_aliases={0: 0, 2: 1},
        compiler_params=params,
        name="insert",
    )(encoded, other, kernel)
    gathered = gather(encoded)
    half, encoded, following, other_edge, factors = pl.pallas_call(
        functools.partial(half_kernel, slots, waves, ka_count, al_count),
        out_shape=(state, sent, edge, edge, shape((4 * slots + 16, lanes), f32)),
        in_specs=[vmem] * 8,
        out_specs=(vmem,) * 5,
        compiler_params=params,
        name="half",
    )(held, m_counts[None], vector_potential, psi, gathered, first_edge, second_edge, kernel)
    gathered = gather(encoded)
    first_edge, second_edge = exchange(following, other_edge)
    term = pl.pallas_call(
        functools.partial(product_kernel, slots, ka_count),
        out_shape=state,
        in_specs=[vmem] * 2,
        out_specs=vmem,
        compiler_params=params,
        cost_estimate=pl.CostEstimate(
            flops=2 * slots * rows * radial_count * lanes * 8, bytes_accessed=4 * 1024 * 1024, transcendentals=0
        ),
        name="product",
    )(gathered, kernel)
    return pl.pallas_call(
        functools.partial(last_kernel, slots, radial_count),
        out_shape=state,
        in_specs=[vmem] * 6,
        out_specs=hbm,
        scratch_shapes=[pltpu.VMEM((slots, rows, lanes), f32), sems],
        compiler_params=params,
        name="last",
    )(factors, psi, half, term, first_edge, second_edge)


def solution(mesh):
    in_specs = (P("al", "ka", None), P("al", "ka", None), P("al"), P(), P())
    out_specs = P("al", "ka", None)
    body = functools.partial(shards, mesh.shape["al"], mesh.shape["ka"])
    return jax.shard_map(body, mesh=mesh, in_specs=in_specs, out_specs=out_specs, check_vma=False)
```

```python
import functools

import jax
import jax.numpy as jnp
from jax import lax
from jax.experimental import pallas as pl
from jax.experimental.pallas import tpu as pltpu
from jax.sharding import PartitionSpec as P

step_length = 0.2
momentum_top = 3.0
TOP = 13
VMEM_LIMIT = 32 * 1024 * 1024


def encode(rounded, out_ref, slot):
    rows = rounded.shape[0]
    values = rounded.astype(jnp.float32)
    largest = jnp.max(jnp.abs(values), axis=0, keepdims=True)
    exponent = jnp.clip(jnp.floor(jnp.log2(jnp.maximum(largest, 1e-36))), -110.0, 127.0)
    scaled = values * jnp.exp2(TOP - exponent)
    out_ref[slot * rows : (slot + 1) * rows, :] = scaled.astype(out_ref.dtype)
    return exponent


def store_exponents(exponents, out_ref, start):
    lanes = exponents[0].shape[1]
    pad = out_ref.shape[0] - start - len(exponents)
    rows = jnp.concatenate(exponents + [jnp.zeros((pad, lanes), jnp.float32)], axis=0)
    out_ref[start:, :] = rows.astype(out_ref.dtype)


def is_even():
    return (lax.axis_index("al") & 1) == 0


def edges_of(first_ref, second_ref):
    first, second = first_ref[...].astype(jnp.float32), second_ref[...].astype(jnp.float32)
    even = is_even()
    return jnp.where(even, second, first), jnp.where(even, first, second)


def encode_kernel(slots, length_ref, psi_in, out_ref, next_ref, other_ref, psi_ref, held_ref):
    rows = psi_ref.shape[1]
    length = scalar(length_ref[...].astype(jnp.float32))
    held_ref[...] = jnp.full(held_ref.shape, length.astype(jnp.float32)).astype(held_ref.dtype)
    exponents = []
    for slot in range(slots):
        psi_ref[slot] = psi_in[slot]
        rounded = psi_in[slot].astype(jnp.bfloat16)
        exponents.append(encode(rounded, out_ref, slot))
    store_exponents(exponents, out_ref, slots * rows)
    high = length - 1
    even = is_even()
    next_ref[...] = psi_in[jnp.where(even, high, 0)].astype(jnp.bfloat16)
    other_ref[...] = psi_in[jnp.where(even, 0, high)].astype(jnp.bfloat16)


def insert_kernel(encoded_ref, other_ref, kernel_in, out_ref, kernel_out):
    count = encoded_ref.shape[0] - 16
    tail = encoded_ref[count:, :].astype(jnp.float32)
    row = lax.broadcasted_iota(jnp.int32, tail.shape, 0)
    tail = jnp.where(row >= 8, other_ref[0:1].astype(jnp.float32), tail)
    out_ref[count:, :] = tail.astype(out_ref.dtype)


def kernel_product(slot, rows, blocks, gathered_ref, kernel_ref, scales):
    total = None
    for pair in range(0, blocks, 2):
        pieces = []
        for block in (pair, pair + 1):
            piece = gathered_ref[block, slot * rows : (slot + 1) * rows, :]
            scale = scales[block][slot : slot + 1]
            pieces.append((piece.astype(jnp.float32) * scale).astype(jnp.bfloat16))
        part = jnp.dot(
            kernel_ref[slot, :, pair * rows : (pair + 2) * rows],
            jnp.concatenate(pieces, axis=0),
            preferred_element_type=jnp.float32,
        )
        total = part if total is None else total + part
    return total


def read_scales(start, blocks, gathered_ref):
    return [
        jnp.exp2(gathered_ref[b, start : start + 16, :].astype(jnp.float32) - TOP)
        for b in range(blocks)
    ]


def scalar(row):
    return jnp.max(row).astype(jnp.int32)


def coupling_factors(slots, waves, first, counts, lanes):
    shape = (4 * slots, lanes)
    row = lax.broadcasted_iota(jnp.int32, shape, 0)
    lane = lax.broadcasted_iota(jnp.int32, shape, 1)
    slot, kind = row >> 2, row & 3
    q = jnp.where(lane < lanes // 2, lane, lane - lanes // 2)

    def pick(offset):
        value = jnp.full(shape, counts[offset], jnp.int32)
        for s in range(1, slots):
            value = jnp.where(slot == s, counts[s + offset], value)
        return value

    is_low = (kind & 1) == 0
    is_up = kind < 2
    count = pick(1)
    source = jnp.where(is_low, pick(0), pick(2))
    wave = first + slot
    other = wave + jnp.where(is_low, -1, 1)
    present = (other >= 0) & (other < waves)
    center = (count - 1) >> 1
    p = q + ((source - 1) >> 1) - center - jnp.where(is_up, 1, -1)
    allowed = (q < count) & (p >= 0) & (p < source) & present
    n = (q - center - jnp.where(is_up, 1, 0)).astype(jnp.float32)
    v = (wave + jnp.where(is_up, jnp.where(is_low, -1, 1), 0)).astype(jnp.float32)
    rises = (kind == 0) | (kind == 3)
    top = jnp.where(rises, (v + n + 1.0) * (v + n + 2.0), (v - n) * (v - n - 1.0))
    bottom = (2.0 * v + 1.0) * jnp.where(rises, 2.0 * v + 3.0, 2.0 * v - 1.0)
    size = jnp.sqrt(jnp.maximum(top, 0.0) / jnp.maximum(bottom, 1.0))
    return jnp.where(allowed, jnp.where(rises, size, -size), 0.0)


def lane_masks(slots, held, counts, lanes):
    lane = lax.broadcasted_iota(jnp.int32, (1, lanes), 1)
    q = jnp.where(lane < lanes // 2, lane, lane - lanes // 2)
    return [(q < counts[s + 1]) & (s < held) for s in range(slots)]


def coupled(slot, slots, held, counts, factors, states, lowest, highest):
    lanes = lowest.shape[1]
    below = lowest if slot == 0 else states[slot - 1]
    above = highest if slot == slots - 1 else jnp.where(slot + 1 < held, states[slot + 1], highest)
    center = (counts[slot + 1] - 1) >> 1
    sums = []
    for change, kind in ((1, 0), (-1, 2)):
        total = None
        for source, offset in ((below, 0), (above, 1)):
            shift = ((counts[slot + 2 * offset] - 1) >> 1) - center - change
            turned = pltpu.roll(source, (2 * lanes - shift) & (lanes - 1), 1)
            row = 4 * slot + kind + offset
            term = factors[row : row + 1] * turned
            total = term if total is None else total + term
        sums.append(total)
    return sums


def flow_of(current, term, up, down, field_x, field_y, momenta, kinetic):
    lanes = current.shape[1]
    lane = lax.broadcasted_iota(jnp.int32, (1, lanes), 1)
    turn = kinetic * current + term + momenta * (field_x * (up + down))
    swapped = pltpu.roll(turn, lanes // 2, 1)
    swapped = jnp.where(lane < lanes // 2, swapped, -swapped)
    return swapped + momenta * (field_y * (down - up))


def momenta_of(rows, lanes, radial_count):
    row = lax.broadcasted_iota(jnp.int32, (rows, lanes), 0) + lax.axis_index("ka") * rows
    momenta = (row.astype(jnp.float32) + 0.5) * (momentum_top / radial_count)
    return momenta, 0.5 * (momenta * momenta)


def half_kernel(
    slots, waves, blocks, al_count,
    held_ref, counts_ref, field_ref, psi_ref, gathered_ref, first_ref, second_ref, kernel_ref,
    half_ref, out_ref, next_ref, other_ref, factor_ref,
):
    rows, lanes = psi_ref.shape[1:]
    start = slots * rows
    seen = None
    for block in range(blocks):
        row = gathered_ref[block, start : start + 16, :].astype(jnp.float32)[8:9]
        seen = row if seen is None else seen + row
    seen = scalar(seen)
    held = scalar(held_ref[0:1].astype(jnp.float32))
    first = jnp.where(2 * lax.axis_index("al") < al_count, seen, waves - held - seen)
    lane = lax.broadcasted_iota(jnp.int32, (1, lanes), 1)
    known = jnp.concatenate(
        [counts_ref[...].astype(jnp.float32), jnp.zeros((1, lanes - waves), jnp.float32)], axis=1
    )
    counts = [
        scalar(jnp.where(lane == jnp.clip(first - 1 + i, 0, waves - 1), known, 0.0))
        for i in range(slots + 2)
    ]
    factors = coupling_factors(slots, waves, first, counts, lanes)
    notes = jnp.full((16, lanes), held.astype(jnp.float32))
    line = lax.broadcasted_iota(jnp.int32, (16, lanes), 0)
    for i in range(slots + 2):
        notes = jnp.where(line == i, counts[i].astype(jnp.float32), notes)
    halves = [
        jnp.broadcast_to(0.5 * field_ref[section : section + 1, part : part + 1], (1, lanes))
        for section in range(2)
        for part in range(2)
    ]
    for i in range(2):
        notes = jnp.where(line == 8 + i, halves[2 + i], notes)
    factor_ref[...] = jnp.concatenate([factors, notes], axis=0)
    masks = lane_masks(slots, held, counts, lanes)
    momenta, kinetic = momenta_of(rows, lanes, kernel_ref.shape[2])
    scales = read_scales(start, blocks, gathered_ref)
    psi = [jnp.where(masks[s], psi_ref[s], 0.0) for s in range(slots)]
    lowest, highest = edges_of(first_ref, second_ref)
    exponents = []
    for slot in range(slots):
        up, down = coupled(slot, slots, held, counts, factors, psi, lowest, highest)
        term = kernel_product(slot, rows, blocks, gathered_ref, kernel_ref, scales)
        flow = flow_of(psi[slot], term, up, down, halves[0], halves[1], momenta, kinetic)
        half = jnp.where(masks[slot], psi[slot] + (0.5 * step_length) * flow, 0.0)
        half_ref[slot] = half
        rounded = half.astype(jnp.bfloat16)
        exponents.append(encode(rounded, out_ref, slot))
    store_exponents(exponents, out_ref, start)
    even = is_even()
    next_ref[...] = half_ref[jnp.where(even, held - 1, 0)].astype(jnp.bfloat16)
    other_ref[...] = half_ref[jnp.where(even, 0, held - 1)].astype(jnp.bfloat16)


def product_kernel(slots, blocks, gathered_ref, kernel_ref, out_ref):
    rows = out_ref.shape[1]
    scales = read_scales(slots * rows, blocks, gathered_ref)
    for slot in range(slots):
        out_ref[slot] = kernel_product(slot, rows, blocks, gathered_ref, kernel_ref, scales)


def last_kernel(
    slots, radial_count, factor_ref, psi_ref, half_ref, term_ref, first_ref, second_ref,
    out_hbm, out_ref, sems,
):
    rows, lanes = psi_ref.shape[1:]
    base = 4 * slots
    counts = [scalar(factor_ref[base + i : base + i + 1]) for i in range(slots + 2)]
    held = scalar(factor_ref[base + slots + 2 : base + slots + 3])
    factors = factor_ref[0:base]
    fields = factor_ref[base + 8 : base + 9], factor_ref[base + 9 : base + 10]
    masks = lane_masks(slots, held, counts, lanes)
    momenta, kinetic = momenta_of(rows, lanes, radial_count)
    lowest, highest = edges_of(first_ref, second_ref)
    states = [half_ref[s] for s in range(slots)]
    copies = []
    for slot in range(slots):
        up, down = coupled(slot, slots, held, counts, factors, states, lowest, highest)
        flow = flow_of(states[slot], term_ref[slot], up, down, *fields, momenta, kinetic)
        out_ref[slot] = jnp.where(masks[slot], psi_ref[slot] + step_length * flow, 0.0)
        copies.append(pltpu.make_async_copy(out_ref.at[slot], out_hbm.at[slot], sems.at[slot]))
        copies[slot].start()
    for copy in copies:
        copy.wait()


def shards(al_count, ka_count, amplitudes, kernel, block_lengths, m_counts, vector_potential):
    slots, rows, lanes = amplitudes.shape
    radial_count = kernel.shape[2]
    waves = m_counts.shape[0]
    sent_rows = slots * rows + 16
    vmem = pl.BlockSpec(memory_space=pltpu.VMEM)
    hbm = pl.BlockSpec(memory_space=pltpu.HBM)
    params = pltpu.CompilerParams(vmem_limit_bytes=VMEM_LIMIT)
    f32, bf16 = jnp.float32, jnp.bfloat16
    shape = jax.ShapeDtypeStruct
    edge = shape((rows, lanes), bf16)
    sent = shape((sent_rows, lanes), bf16)
    state = shape((slots, rows, lanes), f32)
    sems = pltpu.SemaphoreType.DMA((slots,))

    route = []
    for target in range(al_count // 2):
        for source in range(target):
            route.append((source * ka_count + target - 1, target * ka_count + source))
            source_twin, target_twin = al_count - 1 - source, al_count - 1 - target
            route.append((source_twin * ka_count + target - 1, target_twin * ka_count + source))
    def pairs(start):
        return [(i + a, i + 1 - a) for i in range(start, al_count - 1, 2) for a in (0, 1)]

    def exchange(following, other):
        return lax.ppermute(following, "al", pairs(0)), lax.ppermute(other, "al", pairs(1))

    def gather(payload):
        payload = lax.optimization_barrier(payload.astype(jnp.float16))
        everything = lax.optimization_barrier(lax.all_gather(payload, "ka", axis=0, tiled=False))
        return everything.astype(bf16)

    encoded, following, other_edge, psi, held = pl.pallas_call(
        functools.partial(encode_kernel, slots),
        out_shape=(sent, edge, edge, state, shape((16, lanes), bf16)),
        in_specs=[vmem] * 2,
        out_specs=(vmem,) * 5,
        compiler_params=params,
        name="encode",
    )(block_lengths[None], amplitudes)
    other = lax.ppermute(held, ("al", "ka"), route)
    first_edge, second_edge = exchange(following, other_edge)
    encoded, kernel = pl.pallas_call(
        insert_kernel,
        out_shape=(sent, shape(kernel.shape, bf16)),
        in_specs=[vmem] * 3,
        out_specs=(vmem,) * 2,
        input_output_aliases={0: 0, 2: 1},
        compiler_params=params,
        name="insert",
    )(encoded, other, kernel)
    gathered = gather(encoded)
    half, encoded, following, other_edge, factors = pl.pallas_call(
        functools.partial(half_kernel, slots, waves, ka_count, al_count),
        out_shape=(state, sent, edge, edge, shape((4 * slots + 16, lanes), f32)),
        in_specs=[vmem] * 8,
        out_specs=(vmem,) * 5,
        compiler_params=params,
        name="half",
    )(held, m_counts[None], vector_potential, psi, gathered, first_edge, second_edge, kernel)
    gathered = gather(encoded)
    first_edge, second_edge = exchange(following, other_edge)
    term = pl.pallas_call(
        functools.partial(product_kernel, slots, ka_count),
        out_shape=state,
        in_specs=[vmem] * 2,
        out_specs=vmem,
        compiler_params=params,
        cost_estimate=pl.CostEstimate(
            flops=2 * slots * rows * radial_count * lanes * 8, bytes_accessed=4 * 1024 * 1024, transcendentals=0
        ),
        name="product",
    )(gathered, kernel)
    return pl.pallas_call(
        functools.partial(last_kernel, slots, radial_count),
        out_shape=state,
        in_specs=[vmem] * 6,
        out_specs=hbm,
        scratch_shapes=[pltpu.VMEM((slots, rows, lanes), f32), sems],
        compiler_params=params,
        name="last",
    )(factors, psi, half, term, first_edge, second_edge)


def solution(mesh):
    in_specs = (P("al", "ka", None), P("al", "ka", None), P("al"), P(), P())
    out_specs = P("al", "ka", None)
    body = functools.partial(shards, mesh.shape["al"], mesh.shape["ka"])
    return jax.shard_map(body, mesh=mesh, in_specs=in_specs, out_specs=out_specs, check_vma=False)
```

```python
import functools

import jax
import jax.numpy as jnp
from jax import lax
from jax.experimental import pallas as pl
from jax.experimental.pallas import tpu as pltpu
from jax.sharding import PartitionSpec as P

step_length = 0.2
momentum_top = 3.0
TOP = 13
VMEM_LIMIT = 32 * 1024 * 1024


def encode(rounded, out_ref, slot):
    rows = rounded.shape[0]
    values = rounded.astype(jnp.float32)
    largest = jnp.max(jnp.abs(values), axis=0, keepdims=True)
    exponent = jnp.clip(jnp.floor(jnp.log2(jnp.maximum(largest, 1e-36))), -110.0, 127.0)
    scaled = values * jnp.exp2(TOP - exponent)
    out_ref[slot * rows : (slot + 1) * rows, :] = scaled.astype(out_ref.dtype)
    return exponent


def store_exponents(exponents, out_ref, start):
    lanes = exponents[0].shape[1]
    pad = out_ref.shape[0] - start - len(exponents)
    rows = jnp.concatenate(exponents + [jnp.zeros((pad, lanes), jnp.float32)], axis=0)
    out_ref[start:, :] = rows.astype(out_ref.dtype)


def is_even():
    return (lax.axis_index("al") & 1) == 0


def edges_of(first_ref, second_ref):
    first, second = first_ref[...].astype(jnp.float32), second_ref[...].astype(jnp.float32)
    even = is_even()
    return jnp.where(even, second, first), jnp.where(even, first, second)


def encode_kernel(slots, length_ref, psi_in, out_ref, next_ref, other_ref, psi_ref, held_ref):
    rows = psi_ref.shape[1]
    length = scalar(length_ref[...].astype(jnp.float32))
    held_ref[...] = jnp.full(held_ref.shape, length.astype(jnp.float32)).astype(held_ref.dtype)
    exponents = []
    for slot in range(slots):
        psi_ref[slot] = psi_in[slot]
        rounded = psi_in[slot].astype(jnp.bfloat16)
        exponents.append(encode(rounded, out_ref, slot))
    store_exponents(exponents, out_ref, slots * rows)
    high = length - 1
    even = is_even()
    next_ref[...] = psi_in[jnp.where(even, high, 0)].astype(jnp.bfloat16)
    other_ref[...] = psi_in[jnp.where(even, 0, high)].astype(jnp.bfloat16)


def insert_kernel(encoded_ref, other_ref, kernel_in, out_ref, kernel_out):
    count = encoded_ref.shape[0] - 16
    tail = encoded_ref[count:, :].astype(jnp.float32)
    row = lax.broadcasted_iota(jnp.int32, tail.shape, 0)
    tail = jnp.where(row >= 8, other_ref[0:1].astype(jnp.float32), tail)
    out_ref[count:, :] = tail.astype(out_ref.dtype)


def kernel_product(slot, rows, blocks, gathered_ref, kernel_ref, scales):
    total = None
    for pair in range(0, blocks, 2):
        pieces = []
        for block in (pair, pair + 1):
            piece = gathered_ref[block, slot * rows : (slot + 1) * rows, :]
            scale = scales[block][slot : slot + 1]
            pieces.append((piece.astype(jnp.float32) * scale).astype(jnp.bfloat16))
        part = jnp.dot(
            kernel_ref[slot, :, pair * rows : (pair + 2) * rows],
            jnp.concatenate(pieces, axis=0),
            preferred_element_type=jnp.float32,
        )
        total = part if total is None else total + part
    return total


def read_scales(start, blocks, gathered_ref):
    return [
        jnp.exp2(gathered_ref[b, start : start + 16, :].astype(jnp.float32) - TOP)
        for b in range(blocks)
    ]


def scalar(row):
    return jnp.max(row).astype(jnp.int32)


def coupling_factors(slots, waves, first, counts, lanes):
    shape = (4 * slots, lanes)
    row = lax.broadcasted_iota(jnp.int32, shape, 0)
    lane = lax.broadcasted_iota(jnp.int32, shape, 1)
    slot, kind = row >> 2, row & 3
    q = jnp.where(lane < lanes // 2, lane, lane - lanes // 2)

    def pick(offset):
        value = jnp.full(shape, counts[offset], jnp.int32)
        for s in range(1, slots):
            value = jnp.where(slot == s, counts[s + offset], value)
        return value

    is_low = (kind & 1) == 0
    is_up = kind < 2
    count = pick(1)
    source = jnp.where(is_low, pick(0), pick(2))
    wave = first + slot
    other = wave + jnp.where(is_low, -1, 1)
    present = (other >= 0) & (other < waves)
    center = (count - 1) >> 1
    p = q + ((source - 1) >> 1) - center - jnp.where(is_up, 1, -1)
    allowed = (q < count) & (p >= 0) & (p < source) & present
    n = (q - center - jnp.where(is_up, 1, 0)).astype(jnp.float32)
    v = (wave + jnp.where(is_up, jnp.where(is_low, -1, 1), 0)).astype(jnp.float32)
    rises = (kind == 0) | (kind == 3)
    top = jnp.where(rises, (v + n + 1.0) * (v + n + 2.0), (v - n) * (v - n - 1.0))
    bottom = (2.0 * v + 1.0) * jnp.where(rises, 2.0 * v + 3.0, 2.0 * v - 1.0)
    size = jnp.sqrt(jnp.maximum(top, 0.0) / jnp.maximum(bottom, 1.0))
    return jnp.where(allowed, jnp.where(rises, size, -size), 0.0)


def lane_masks(slots, held, counts, lanes):
    lane = lax.broadcasted_iota(jnp.int32, (1, lanes), 1)
    q = jnp.where(lane < lanes // 2, lane, lane - lanes // 2)
    return [(q < counts[s + 1]) & (s < held) for s in range(slots)]


def coupled(slot, slots, held, counts, factors, states, lowest, highest):
    lanes = lowest.shape[1]
    below = lowest if slot == 0 else states[slot - 1]
    above = highest if slot == slots - 1 else jnp.where(slot + 1 < held, states[slot + 1], highest)
    center = (counts[slot + 1] - 1) >> 1
    sums = []
    for change, kind in ((1, 0), (-1, 2)):
        total = None
        for source, offset in ((below, 0), (above, 1)):
            shift = ((counts[slot + 2 * offset] - 1) >> 1) - center - change
            turned = pltpu.roll(source, (2 * lanes - shift) & (lanes - 1), 1)
            row = 4 * slot + kind + offset
            term = factors[row : row + 1] * turned
            total = term if total is None else total + term
        sums.append(total)
    return sums


def flow_of(current, term, up, down, field_x, field_y, momenta, kinetic):
    lanes = current.shape[1]
    lane = lax.broadcasted_iota(jnp.int32, (1, lanes), 1)
    turn = kinetic * current + term + momenta * (field_x * (up + down))
    swapped = pltpu.roll(turn, lanes // 2, 1)
    swapped = jnp.where(lane < lanes // 2, swapped, -swapped)
    return swapped + momenta * (field_y * (down - up))


def momenta_of(rows, lanes, radial_count):
    row = lax.broadcasted_iota(jnp.int32, (rows, lanes), 0) + lax.axis_index("ka") * rows
    momenta = (row.astype(jnp.float32) + 0.5) * (momentum_top / radial_count)
    return momenta, 0.5 * (momenta * momenta)


def half_kernel(
    slots, waves, blocks, al_count,
    held_ref, counts_ref, field_ref, psi_ref, gathered_ref, first_ref, second_ref, kernel_ref,
    half_ref, out_ref, next_ref, other_ref, factor_ref,
):
    rows, lanes = psi_ref.shape[1:]
    start = slots * rows
    seen = None
    for block in range(blocks):
        row = gathered_ref[block, start : start + 16, :].astype(jnp.float32)[8:9]
        seen = row if seen is None else seen + row
    seen = scalar(seen)
    held = scalar(held_ref[0:1].astype(jnp.float32))
    first = jnp.where(2 * lax.axis_index("al") < al_count, seen, waves - held - seen)
    lane = lax.broadcasted_iota(jnp.int32, (1, lanes), 1)
    known = jnp.concatenate(
        [counts_ref[...].astype(jnp.float32), jnp.zeros((1, lanes - waves), jnp.float32)], axis=1
    )
    counts = [
        scalar(jnp.where(lane == jnp.clip(first - 1 + i, 0, waves - 1), known, 0.0))
        for i in range(slots + 2)
    ]
    factors = coupling_factors(slots, waves, first, counts, lanes)
    notes = jnp.full((16, lanes), held.astype(jnp.float32))
    line = lax.broadcasted_iota(jnp.int32, (16, lanes), 0)
    for i in range(slots + 2):
        notes = jnp.where(line == i, counts[i].astype(jnp.float32), notes)
    halves = [
        jnp.broadcast_to(0.5 * field_ref[section : section + 1, part : part + 1], (1, lanes))
        for section in range(2)
        for part in range(2)
    ]
    for i in range(2):
        notes = jnp.where(line == 8 + i, halves[2 + i], notes)
    factor_ref[...] = jnp.concatenate([factors, notes], axis=0)
    masks = lane_masks(slots, held, counts, lanes)
    momenta, kinetic = momenta_of(rows, lanes, kernel_ref.shape[2])
    scales = read_scales(start, blocks, gathered_ref)
    psi = [jnp.where(masks[s], psi_ref[s], 0.0) for s in range(slots)]
    lowest, highest = edges_of(first_ref, second_ref)
    exponents = []
    for slot in range(slots):
        up, down = coupled(slot, slots, held, counts, factors, psi, lowest, highest)
        term = kernel_product(slot, rows, blocks, gathered_ref, kernel_ref, scales)
        flow = flow_of(psi[slot], term, up, down, halves[0], halves[1], momenta, kinetic)
        half = jnp.where(masks[slot], psi[slot] + (0.5 * step_length) * flow, 0.0)
        half_ref[slot] = half
        rounded = half.astype(jnp.bfloat16)
        exponents.append(encode(rounded, out_ref, slot))
    store_exponents(exponents, out_ref, start)
    even = is_even()
    next_ref[...] = half_ref[jnp.where(even, held - 1, 0)].astype(jnp.bfloat16)
    other_ref[...] = half_ref[jnp.where(even, 0, held - 1)].astype(jnp.bfloat16)


def last_kernel(
    slots, blocks, radial_count, factor_ref, psi_ref, half_ref, gathered_ref, kernel_ref, first_ref, second_ref,
    out_hbm, out_ref, sems,
):
    rows, lanes = psi_ref.shape[1:]
    base = 4 * slots
    counts = [scalar(factor_ref[base + i : base + i + 1]) for i in range(slots + 2)]
    held = scalar(factor_ref[base + slots + 2 : base + slots + 3])
    factors = factor_ref[0:base]
    fields = factor_ref[base + 8 : base + 9], factor_ref[base + 9 : base + 10]
    masks = lane_masks(slots, held, counts, lanes)
    momenta, kinetic = momenta_of(rows, lanes, radial_count)
    lowest, highest = edges_of(first_ref, second_ref)
    states = [half_ref[s] for s in range(slots)]
    scales = read_scales(slots * rows, blocks, gathered_ref)
    copies = []
    for slot in range(slots):
        term = kernel_product(slot, rows, blocks, gathered_ref, kernel_ref, scales)
        up, down = coupled(slot, slots, held, counts, factors, states, lowest, highest)
        flow = flow_of(states[slot], term, up, down, *fields, momenta, kinetic)
        out_ref[slot] = jnp.where(masks[slot], psi_ref[slot] + step_length * flow, 0.0)
        copies.append(pltpu.make_async_copy(out_ref.at[slot], out_hbm.at[slot], sems.at[slot]))
        copies[slot].start()
    for copy in copies:
        copy.wait()


def shards(al_count, ka_count, amplitudes, kernel, block_lengths, m_counts, vector_potential):
    slots, rows, lanes = amplitudes.shape
    radial_count = kernel.shape[2]
    waves = m_counts.shape[0]
    sent_rows = slots * rows + 16
    vmem = pl.BlockSpec(memory_space=pltpu.VMEM)
    hbm = pl.BlockSpec(memory_space=pltpu.HBM)
    params = pltpu.CompilerParams(vmem_limit_bytes=VMEM_LIMIT)
    f32, bf16 = jnp.float32, jnp.bfloat16
    shape = jax.ShapeDtypeStruct
    edge = shape((rows, lanes), bf16)
    sent = shape((sent_rows, lanes), bf16)
    state = shape((slots, rows, lanes), f32)
    sems = pltpu.SemaphoreType.DMA((slots,))

    route = []
    for target in range(al_count // 2):
        for source in range(target):
            route.append((source * ka_count + target, target * ka_count + source))
            source_twin, target_twin = al_count - 1 - source, al_count - 1 - target
            route.append((source_twin * ka_count + target, target_twin * ka_count + source))
    def pairs(start):
        return [(i + a, i + 1 - a) for i in range(start, al_count - 1, 2) for a in (0, 1)]

    def exchange(following, other):
        return lax.ppermute(following, "al", pairs(0)), lax.ppermute(other, "al", pairs(1))

    def gather(payload):
        payload = lax.optimization_barrier(payload.astype(jnp.float16))
        everything = lax.optimization_barrier(lax.all_gather(payload, "ka", axis=0, tiled=False))
        return everything.astype(bf16)

    encoded, following, other_edge, psi, held = pl.pallas_call(
        functools.partial(encode_kernel, slots),
        out_shape=(sent, edge, edge, state, shape((16, lanes), bf16)),
        in_specs=[vmem] * 2,
        out_specs=(vmem,) * 5,
        compiler_params=params,
        name="encode",
    )(block_lengths[None], amplitudes)
    other = lax.ppermute(held, ("al", "ka"), route)
    first_edge, second_edge = exchange(following, other_edge)
    encoded, kernel = pl.pallas_call(
        insert_kernel,
        out_shape=(sent, shape(kernel.shape, bf16)),
        in_specs=[vmem] * 3,
        out_specs=(vmem,) * 2,
        input_output_aliases={0: 0, 2: 1},
        compiler_params=params,
        name="insert",
    )(encoded, other, kernel)
    gathered = gather(encoded)
    half, encoded, following, other_edge, factors = pl.pallas_call(
        functools.partial(half_kernel, slots, waves, ka_count, al_count),
        out_shape=(state, sent, edge, edge, shape((4 * slots + 16, lanes), f32)),
        in_specs=[vmem] * 8,
        out_specs=(vmem,) * 5,
        compiler_params=params,
        name="half",
    )(held, m_counts[None], vector_potential, psi, gathered, first_edge, second_edge, kernel)
    gathered = gather(encoded)
    first_edge, second_edge = exchange(following, other_edge)
    return pl.pallas_call(
        functools.partial(last_kernel, slots, ka_count, radial_count),
        out_shape=state,
        in_specs=[vmem] * 7,
        out_specs=hbm,
        scratch_shapes=[pltpu.VMEM((slots, rows, lanes), f32), sems],
        compiler_params=params,
        name="last",
    )(factors, psi, half, gathered, kernel, first_edge, second_edge)


def solution(mesh):
    in_specs = (P("al", "ka", None), P("al", "ka", None), P("al"), P(), P())
    out_specs = P("al", "ka", None)
    body = functools.partial(shards, mesh.shape["al"], mesh.shape["ka"])
    return jax.shard_map(body, mesh=mesh, in_specs=in_specs, out_specs=out_specs, check_vma=False)
```
